32 devices in a mesh: gr: 4 (over y, x), gc: 8 (over z, core).
Axes of the slice: x: 2, y: 2, z: 4, core: 2. Of those that a mesh axis runs over, the one named last changes fastest.
Arguments:
- jacobian: bfloat16 [65536, 1536], P(('gr', 'gc')), may hold values from -0.43164062 to 0.43164062
- class_scores: float32 [192, 8], replicated, may hold values from 0.1 to 10
- source: int32 [32768], replicated, may hold values from 0 to 65535, as said below
Outputs:
- gram_slab: float32 [2048, 32768], P('gr', 'gc')
The draws below stay inside these ranges and needn't reach their ends.
Inputs may be any that keep to these rules, and one draw needn't show every extreme that they name: `source`: entries are distinct. Entry k is o * 2048 + j for owner o (flat index over gr then gc) and local column j. In each aligned tile of 4096 consecutive entries no owner appears more than 192 times, and some owner appears exactly 192 times in every tile.
All inputs are finite; a program needn't handle non-finite values.
Results may differ from the reference program's by a relative error of at most 0.0033.
Values may be sent and summed in bfloat16 or wider, within the bound.
A program may use at most 128 MiB of HBM per device.

```python
import math
import jax
import jax.numpy as jnp
from jax import lax

TOKENS = 192
CLASSES = 8
SELECTED = 32768
ROWS = 1536
PLOC = 2048
PAIR_MEAN = 128
TILE = 4096
SLAB = 2048
N_GC = 8
DEVICES = 32


def draw_source(key, part):
    key = jax.random.fold_in(key, 11)
    key_order, key_spread, key_local, key_shuffle = jax.random.split(key, 4)
    orders = jax.vmap(lambda sub: jax.random.permutation(sub, DEVICES))(jax.random.split(key_order, N_GC))
    halves = DEVICES // 2
    spread = jax.random.randint(key_spread, (N_GC, halves), -(PAIR_MEAN // 2), PAIR_MEAN // 2 + 1)
    spread = spread.at[:, 0].set(PAIR_MEAN // 2)
    paired = jnp.stack([PAIR_MEAN + spread, PAIR_MEAN - spread], axis=-1).reshape(N_GC, DEVICES)
    tile_ids = jnp.arange(N_GC)[:, None]
    counts = jnp.zeros((N_GC, DEVICES), jnp.int32).at[tile_ids, orders].set(paired.astype(jnp.int32))
    labels = jax.vmap(lambda amount: jnp.repeat(jnp.arange(DEVICES, dtype=jnp.int32), amount, total_repeat_length=TILE))(counts)
    starts = jnp.cumsum(counts, axis=1) - counts
    occurrence = jnp.arange(TILE, dtype=jnp.int32)[None, :] - jnp.take_along_axis(starts, labels, axis=1)
    bases = jnp.cumsum(counts, axis=0) - counts
    column_rank = jnp.take_along_axis(bases, labels, axis=1) + occurrence
    owner_perms = jax.vmap(lambda sub: jax.random.permutation(sub, PLOC))(jax.random.split(key_local, DEVICES))
    local_columns = owner_perms[labels, column_rank]
    values = labels * PLOC + local_columns
    shuffles = jax.vmap(lambda sub: jax.random.permutation(sub, TILE))(jax.random.split(key_shuffle, N_GC))
    values = jnp.take_along_axis(values, shuffles, axis=1)
    return values.reshape(-1).astype(jnp.int32)


def block_levels(own_key, extent, cuts, least, largest):
    loudness = 1.0
    for dim, parts in cuts:
        steps = jax.random.uniform(jax.random.fold_in(jax.random.fold_in(own_key, 6), dim), (parts,), jnp.float32, least / len(cuts), largest / len(cuts))
        loudness = loudness * jnp.repeat(jnp.exp(steps), extent[dim] // parts).reshape((-1,) + (1,) * (len(extent) - 1 - dim))
    return loudness


def noise(key, shape, scale, bound, shards=(), kind=jnp.bfloat16):
    entries = scale * jax.random.normal(key, shape, jnp.float32)
    if shards:
        entries = entries * block_levels(key, shape, shards, -0.22, 0.18)
    return jnp.clip(entries, -bound, bound).astype(kind)


def setup_inputs(seed: int = 0) -> dict:
    splits = jax.random.split(jax.random.key(seed), 4)
    jacobian = noise(splits[0], (DEVICES * PLOC, ROWS), (TOKENS ** -0.5), 0.43164062, ((0, 32),))
    class_scores = jnp.clip(jnp.exp(jax.random.uniform(splits[1], (TOKENS, CLASSES), jnp.float32, math.log(0.1), math.log(10.0))), 0.1, 10.0)
    source = draw_source(jax.random.fold_in(splits[3], 71), 0)
    return {"jacobian": jacobian, "class_scores": class_scores, "source": source}


def weigh_rows(block, probs, root):
    values = block.astype(jnp.float32).reshape(block.shape[0], probs.shape[0], probs.shape[1])
    centre = lax.optimization_barrier(jnp.sum(values * probs, axis=-1, keepdims=True))
    return (root * (values - centre)).astype(jnp.bfloat16).reshape(block.shape[0], -1)

def reference(jacobian, class_scores, source):
    probs = class_scores / lax.optimization_barrier(jnp.sum(class_scores, axis=1, keepdims=True))
    root = jnp.sqrt(probs)
    picked = jnp.take(jacobian, source, axis=0)
    weighted = weigh_rows(picked, probs, root)
    slab_part = weighted[SELECTED - SLAB:].astype(jnp.float32)
    positions = SELECTED - SLAB + jnp.arange(SLAB, dtype=jnp.int32)

    def one_block(block_index):
        columns = lax.dynamic_slice_in_dim(weighted, block_index * TILE, TILE, 0).astype(jnp.float32)
        product = jnp.dot(slab_part, columns.T, precision=lax.Precision.HIGHEST)
        column_ids = block_index * TILE + jnp.arange(TILE, dtype=jnp.int32)
        return jnp.where(column_ids[None, :] <= positions[:, None], product, jnp.float32(0.0))
    blocks = lax.map(one_block, jnp.arange(N_GC, dtype=jnp.int32))
    return jnp.transpose(blocks, (1, 0, 2)).reshape(SLAB, SELECTED)
```

```python
import functools

import jax
import jax.numpy as jnp
from jax import lax
from jax.experimental import pallas as pl
from jax.experimental.pallas import tpu as pltpu
from jax.sharding import PartitionSpec as P

SLAB_DEV = 512
GROUP = 256
VMEM_LIMIT = 48 * 1024 * 1024


def pick_kernel(classes, count_rows, width, index_ref, probs_ref, root_ref, jacobian_ref, *rest):
    out_refs, matrix_ref = rest[:-1], rest[-1]
    groups = matrix_ref.shape[1]

    @pl.when(pl.program_id(0) == 0)
    def _():
        down = lax.broadcasted_iota(jnp.int32, (GROUP, GROUP), 0) // classes
        across = lax.broadcasted_iota(jnp.int32, (GROUP, GROUP), 1) // classes
        for g in range(groups):
            exact = jnp.where(down == across, probs_ref[g], 0.0)
            for part in range(3):
                piece = exact.astype(jnp.bfloat16)
                matrix_ref[part, g] = piece
                exact = exact - piece.astype(jnp.float32)

    capacity = index_ref.shape[1]
    local_width = jacobian_ref.shape[0]
    lanes = lax.broadcasted_iota(jnp.int32, (capacity, local_width), 1)
    onehot = jnp.where(lanes == index_ref[0], 1.0, 0.0).astype(jnp.bfloat16)
    pieces = []
    for g in range(groups):
        span = slice(g * GROUP, (g + 1) * GROUP)
        values = jnp.dot(onehot, jacobian_ref[:, span], preferred_element_type=jnp.float32)
        short = values.astype(jnp.bfloat16)
        centre = jnp.dot(short, matrix_ref[2, g], preferred_element_type=jnp.float32)
        centre += jnp.dot(short, matrix_ref[1, g], preferred_element_type=jnp.float32)
        centre += jnp.dot(short, matrix_ref[0, g], preferred_element_type=jnp.float32)
        pieces.append((root_ref[:, span] * (values - centre)).astype(jnp.bfloat16))
    weighted = jnp.concatenate(pieces, axis=1)
    for c, out_ref in enumerate(out_refs):
        for r in range(count_rows):
            start = (r * len(out_refs) + c) * width
            out_ref[r, 0] = weighted[:, start : start + width]


def pick_rows(jacobian, probs, root, send_index, count_rows, chunks):
    count_cols, capacity = send_index.shape
    local_width, all_rows = jacobian.shape
    groups = all_rows // GROUP
    width = all_rows // count_rows // chunks
    shape = jax.ShapeDtypeStruct((count_rows, count_cols, capacity, width), jnp.bfloat16)
    return pl.pallas_call(
        functools.partial(pick_kernel, probs.shape[1], count_rows, width),
        grid=(count_cols,),
        in_specs=[
            pl.BlockSpec((1, capacity, 1), lambda t: (t, 0, 0)),
            pl.BlockSpec((groups, GROUP, 1), lambda t: (0, 0, 0)),
            pl.BlockSpec((1, all_rows), lambda t: (0, 0)),
            pl.BlockSpec((local_width, all_rows), lambda t: (0, 0)),
        ],
        out_specs=[pl.BlockSpec((count_rows, 1, capacity, width), lambda t: (0, t, 0, 0))] * chunks,
        out_shape=[shape] * chunks,
        scratch_shapes=[pltpu.VMEM((3, groups, GROUP, GROUP), jnp.bfloat16)],
        compiler_params=pltpu.CompilerParams(vmem_limit_bytes=VMEM_LIMIT),
    )(
        send_index[:, :, None],
        probs.reshape(groups, GROUP, 1),
        root.reshape(1, all_rows),
        jacobian,
    )


def product_kernel(chunks, offset_ref, *refs):
    slabs, tiles, out_ref = refs[:chunks], refs[chunks : 2 * chunks], refs[-1]
    total = None
    for slab, tile in zip(slabs, tiles):
        part = lax.dot_general(
            slab[...], tile[...], (((1,), (1,)), ((), ())), preferred_element_type=jnp.float32
        )
        total = part if total is None else total + part
    rows = offset_ref[0] + lax.broadcasted_iota(jnp.int32, out_ref.shape, 0)
    columns = (
        offset_ref[1]
        + pl.program_id(0) * out_ref.shape[1]
        + lax.broadcasted_iota(jnp.int32, out_ref.shape, 1)
    )
    out_ref[...] = jnp.where(columns <= rows, total, 0.0)


def product(slabs, tiles, offsets, tile_width):
    chunks = len(slabs)
    depth = slabs[0].shape[1]
    block = 512
    return pl.pallas_call(
        functools.partial(product_kernel, chunks),
        grid=(tile_width // block,),
        in_specs=[pl.BlockSpec(memory_space=pltpu.SMEM)]
        + [pl.BlockSpec((SLAB_DEV, depth), lambda i: (0, 0))] * chunks
        + [pl.BlockSpec((block, depth), lambda i: (i, 0))] * chunks,
        out_specs=pl.BlockSpec((SLAB_DEV, block), lambda i: (0, i)),
        out_shape=jax.ShapeDtypeStruct((SLAB_DEV, tile_width), jnp.float32),
        compiler_params=pltpu.CompilerParams(vmem_limit_bytes=VMEM_LIMIT),
    )(offsets, *slabs, *tiles)


def local(jacobian, class_scores, source):
    count_rows = lax.axis_size("gr")
    count_cols = lax.axis_size("gc")
    grid_row = lax.axis_index("gr")
    grid_col = lax.axis_index("gc")
    myself = grid_row * count_cols + grid_col
    local_width, all_rows = jacobian.shape
    total_weights = source.shape[0]
    tile_width = total_weights // count_cols
    capacity = 3 * (total_weights // (count_cols * count_cols * count_rows)) // 2
    block_rows = all_rows // count_rows
    chunks = block_rows // 128 if block_rows % 128 == 0 else 1
    width = block_rows // chunks
    slab_total = SLAB_DEV * count_rows
    probs = class_scores / jnp.sum(class_scores, axis=1, keepdims=True)
    root = jnp.sqrt(probs)

    tiles = source.reshape(count_cols, tile_width)
    owned = tiles // local_width == myself
    rank = jnp.where(owned, jnp.cumsum(owned.astype(jnp.int32), axis=1) - 1, -1)
    slots = jnp.arange(capacity, dtype=jnp.int32)
    hit = rank[:, None, :] == slots[None, :, None]
    send_index = jnp.sum(jnp.where(hit, (tiles % local_width + 1)[:, None, :], 0), axis=2) - 1
    outgoing = pick_rows(jacobian, probs, root, send_index, count_rows, chunks)

    tile_source = (
        lax.dynamic_slice_in_dim(source, grid_col * tile_width, tile_width, 0) // local_width
    )
    onehot = (
        tile_source[:, None] == jnp.arange(count_rows * count_cols, dtype=jnp.int32)[None, :]
    ).astype(jnp.int32)
    arrival = jnp.sum(jnp.cumsum(onehot, axis=0) * onehot, axis=1) - 1
    flat_index = tile_source * capacity + arrival

    slab_list, tile_list = [], []
    for part in outgoing:
        incoming = lax.all_to_all(
            part.reshape(-1, capacity, width), ("gr", "gc"), split_axis=0, concat_axis=0, tiled=True
        )
        block = incoming.reshape(-1, width).at[flat_index].get(mode="promise_in_bounds")
        full = lax.all_gather(block, "gr", axis=1, tiled=True)
        piece = lax.dynamic_slice_in_dim(
            full, tile_width - slab_total + grid_row * SLAB_DEV, SLAB_DEV, 0
        )
        mine = grid_col == count_cols - 1
        slab_list.append(lax.psum(jnp.where(mine, piece, jnp.zeros_like(piece)), "gc"))
        tile_list.append(full)
    offsets = jnp.stack(
        [total_weights - slab_total + grid_row * SLAB_DEV, grid_col * tile_width]
    ).astype(jnp.int32)
    return product(slab_list, tile_list, offsets, tile_width)


def solution(mesh):
    in_specs = (P(("gr", "gc"), None), P(), P())
    out_specs = P("gr", "gc")
    return jax.shard_map(local, mesh=mesh, in_specs=in_specs, out_specs=out_specs, check_vma=False)
```

```python
import functools

import jax
import jax.numpy as jnp
from jax import lax
from jax.experimental import pallas as pl
from jax.experimental.pallas import tpu as pltpu
from jax.sharding import PartitionSpec as P

SLAB_DEV = 512
GROUP = 256
PICK_ROWS = 768
VMEM_LIMIT = 48 * 1024 * 1024


def pick_kernel(classes, count_rows, index_ref, probs_ref, root_ref, jacobian_ref, *rest):
    out_refs, matrix_ref = rest[:-1], rest[-1]
    groups = matrix_ref.shape[1]

    @pl.when(pl.program_id(0) == 0)
    def _():
        down = lax.broadcasted_iota(jnp.int32, (GROUP, GROUP), 0) // classes
        across = lax.broadcasted_iota(jnp.int32, (GROUP, GROUP), 1) // classes
        for g in range(groups):
            exact = jnp.where(down == across, probs_ref[g], 0.0)
            for part in range(3):
                piece = exact.astype(jnp.bfloat16)
                matrix_ref[part, g] = piece
                exact = exact - piece.astype(jnp.float32)

    steps, capacity = out_refs[0].shape[1:3]
    local_width, all_rows = jacobian_ref.shape
    lanes = lax.broadcasted_iota(jnp.int32, (steps * capacity, local_width), 1)
    onehot = jnp.where(lanes == index_ref[...], 1.0, 0.0).astype(jnp.bfloat16)
    pieces = []
    for g in range(groups):
        span = slice(g * GROUP, (g + 1) * GROUP)
        values = jnp.dot(onehot, jacobian_ref[:, span], preferred_element_type=jnp.float32)
        short = values.astype(jnp.bfloat16)
        centre = jnp.dot(short, matrix_ref[2, g], preferred_element_type=jnp.float32)
        centre += jnp.dot(short, matrix_ref[1, g], preferred_element_type=jnp.float32)
        centre += jnp.dot(short, matrix_ref[0, g], preferred_element_type=jnp.float32)
        pieces.append((root_ref[:, span] * (values - centre)).astype(jnp.bfloat16))
    weighted = jnp.concatenate(pieces, axis=1)
    for r in range(count_rows):
        start = r * (all_rows // count_rows)
        for out_ref in out_refs:
            width = out_ref.shape[3]
            for t in range(steps):
                rows = slice(t * capacity, (t + 1) * capacity)
                out_ref[r, t] = weighted[rows, start : start + width]
            start += width


def pick_rows(jacobian, probs, root, send_index, count_rows, widths):
    count_cols, capacity = send_index.shape
    local_width, all_rows = jacobian.shape
    groups = all_rows // GROUP
    steps = max(1, min(count_cols, PICK_ROWS // capacity))
    shapes = [(count_rows, count_cols, capacity, width) for width in widths]
    return pl.pallas_call(
        functools.partial(pick_kernel, probs.shape[1], count_rows),
        grid=(count_cols // steps,),
        in_specs=[
            pl.BlockSpec((steps * capacity, 1), lambda t: (t, 0)),
            pl.BlockSpec((groups, GROUP, 1), lambda t: (0, 0, 0)),
            pl.BlockSpec((1, all_rows), lambda t: (0, 0)),
            pl.BlockSpec((local_width, all_rows), lambda t: (0, 0)),
        ],
        out_specs=[
            pl.BlockSpec((count_rows, steps, capacity, width), lambda t: (0, t, 0, 0))
            for width in widths
        ],
        out_shape=[jax.ShapeDtypeStruct(shape, jnp.bfloat16) for shape in shapes],
        scratch_shapes=[pltpu.VMEM((3, groups, GROUP, GROUP), jnp.bfloat16)],
        compiler_params=pltpu.CompilerParams(vmem_limit_bytes=VMEM_LIMIT),
    )(
        send_index.reshape(-1, 1),
        probs.reshape(groups, GROUP, 1),
        root.reshape(1, all_rows),
        jacobian,
    )


def product_kernel(chunks, offset_ref, *refs):
    slabs, tiles, out_ref = refs[:chunks], refs[chunks:-1], refs[-1]
    count = slabs[0].shape[0]
    total = None
    for c, slab in enumerate(slabs):
        for d in range(count):
            part = lax.dot_general(
                slab[d],
                tiles[c * count + d][...],
                (((1,), (1,)), ((), ())),
                preferred_element_type=jnp.float32,
            )
            total = part if total is None else total + part
    rows = offset_ref[0] + lax.broadcasted_iota(jnp.int32, out_ref.shape, 0)
    columns = (
        offset_ref[1]
        + pl.program_id(0) * out_ref.shape[1]
        + lax.broadcasted_iota(jnp.int32, out_ref.shape, 1)
    )
    out_ref[...] = jnp.where(columns <= rows, total, 0.0)


def product(slabs, tiles, offsets, tile_width):
    block = 512
    return pl.pallas_call(
        functools.partial(product_kernel, len(slabs)),
        grid=(tile_width // block,),
        in_specs=[pl.BlockSpec(memory_space=pltpu.SMEM)]
        + [pl.BlockSpec(slab.shape, lambda i: (0, 0, 0)) for slab in slabs]
        + [pl.BlockSpec((block, tile.shape[1]), lambda i: (i, 0)) for tile in tiles],
        out_specs=pl.BlockSpec((SLAB_DEV, block), lambda i: (0, i)),
        out_shape=jax.ShapeDtypeStruct((SLAB_DEV, tile_width), jnp.float32),
        compiler_params=pltpu.CompilerParams(vmem_limit_bytes=VMEM_LIMIT),
    )(offsets, *slabs, *tiles)


def exchange(x, count, d):
    return lax.ppermute(x, "gr", [(i, i ^ d) for i in range(count)])


def gather_pieces(block, count):
    if count != 4:
        return [block] + [exchange(block, count, d) for d in range(1, count)]
    half = block.shape[0] // 2
    one, two = exchange(block, 4, 1), exchange(block, 4, 2)
    top, bottom = exchange(one[:half], 4, 2), exchange(two[half:], 4, 1)
    return [block, one, two, jnp.concatenate([top, bottom])]


def spread_slab(block, count_rows, count_cols, grid_row, grid_col):
    first = block.shape[0] - SLAB_DEV * count_rows
    last = count_cols - 1

    def rows_of(r):
        return lax.dynamic_slice_in_dim(block, first + r * SLAB_DEV, SLAB_DEV, 0)

    own = rows_of(grid_row)
    parts = [jnp.where(grid_col == last, own, jnp.zeros_like(own))]
    for d in range(1, count_rows):
        pairs = [
            (r * count_cols + last, (r ^ d) * count_cols + last) for r in range(count_rows)
        ]
        parts.append(lax.ppermute(rows_of(grid_row ^ d), ("gr", "gc"), pairs))
    slab = jnp.stack(parts)
    stride = count_cols // 2
    while stride:
        pairs = [(c, c - stride) for c in range(last, 0, -2 * stride)]
        slab = slab + lax.ppermute(slab, "gc", pairs)
        stride //= 2
    return slab


def local(jacobian, class_scores, source):
    count_rows = lax.axis_size("gr")
    count_cols = lax.axis_size("gc")
    grid_row = lax.axis_index("gr")
    grid_col = lax.axis_index("gc")
    myself = grid_row * count_cols + grid_col
    local_width, all_rows = jacobian.shape
    total_weights = source.shape[0]
    tile_width = total_weights // count_cols
    capacity = 3 * (total_weights // (count_cols * count_cols * count_rows)) // 2
    block_rows = all_rows // count_rows
    widths = [block_rows]
    if block_rows % 384 == 0:
        widths = [2 * block_rows // 3, block_rows // 3]
    slab_total = SLAB_DEV * count_rows
    probs = class_scores / jnp.sum(class_scores, axis=1, keepdims=True)
    root = jnp.sqrt(probs)

    tiles = source.reshape(count_cols, tile_width)
    owned = tiles // local_width == myself
    rank = jnp.where(owned, jnp.cumsum(owned.astype(jnp.int32), axis=1) - 1, -1)
    slots = jnp.arange(capacity, dtype=jnp.int32)
    hit = rank[:, None, :] == slots[None, :, None]
    send_index = jnp.sum(jnp.where(hit, (tiles % local_width + 1)[:, None, :], 0), axis=2) - 1
    outgoing = pick_rows(jacobian, probs, root, send_index, count_rows, widths)

    tile_source = (
        lax.dynamic_slice_in_dim(source, grid_col * tile_width, tile_width, 0) // local_width
    )
    onehot = (
        tile_source[:, None] == jnp.arange(count_rows * count_cols, dtype=jnp.int32)[None, :]
    ).astype(jnp.int32)
    arrival = jnp.sum(jnp.cumsum(onehot, axis=0) * onehot, axis=1) - 1
    flat_index = tile_source * capacity + arrival

    slab_list, tile_list = [], []
    for part, width in zip(outgoing, widths):
        incoming = lax.all_to_all(
            part.reshape(-1, capacity, width), ("gr", "gc"), split_axis=0, concat_axis=0, tiled=True
        )
        block = incoming.reshape(-1, width).at[flat_index].get(mode="promise_in_bounds")
        tile_list += gather_pieces(block, count_rows)
        slab_list.append(spread_slab(block, count_rows, count_cols, grid_row, grid_col))
    offsets = jnp.stack(
        [total_weights - slab_total + grid_row * SLAB_DEV, grid_col * tile_width]
    ).astype(jnp.int32)
    return product(slab_list, tile_list, offsets, tile_width)


def solution(mesh):
    in_specs = (P(("gr", "gc"), None), P(), P())
    out_specs = P("gr", "gc")
    return jax.shard_map(local, mesh=mesh, in_specs=in_specs, out_specs=out_specs, check_vma=False)
```

```python
import functools

import jax
import jax.numpy as jnp
from jax import lax
from jax.experimental import pallas as pl
from jax.experimental.pallas import tpu as pltpu
from jax.sharding import PartitionSpec as P

SLAB_DEV = 512
PICK_ROWS = 768
VMEM_LIMIT = 48 * 1024 * 1024


def pick_kernel(classes, offset, index_ref, probs_ref, root_ref, jacobian_ref, out_ref, matrix_ref):
    count_rows, steps, capacity, width = out_ref.shape
    local_width, all_rows = jacobian_ref.shape
    spans = [
        slice(r * (all_rows // count_rows) + offset, r * (all_rows // count_rows) + offset + width)
        for r in range(count_rows)
    ]

    @pl.when(pl.program_id(0) == 0)
    def _():
        down = lax.broadcasted_iota(jnp.int32, (width, width), 0) // classes
        across = lax.broadcasted_iota(jnp.int32, (width, width), 1) // classes
        for r, span in enumerate(spans):
            exact = jnp.where(down == across, probs_ref[span], 0.0)
            for part in range(3):
                piece = exact.astype(jnp.bfloat16)
                matrix_ref[part, r] = piece
                exact = exact - piece.astype(jnp.float32)

    lanes = lax.broadcasted_iota(jnp.int32, (steps * capacity, local_width), 1)
    onehot = jnp.where(lanes == index_ref[...], 1.0, 0.0).astype(jnp.bfloat16)
    for r, span in enumerate(spans):
        values = jnp.dot(onehot, jacobian_ref[:, span], preferred_element_type=jnp.float32)
        short = values.astype(jnp.bfloat16)
        centre = jnp.dot(short, matrix_ref[2, r], preferred_element_type=jnp.float32)
        centre += jnp.dot(short, matrix_ref[1, r], preferred_element_type=jnp.float32)
        centre += jnp.dot(short, matrix_ref[0, r], preferred_element_type=jnp.float32)
        weighted = (root_ref[:, span] * (values - centre)).astype(jnp.bfloat16)
        for t in range(steps):
            out_ref[r, t] = weighted[t * capacity : (t + 1) * capacity]


def pick_rows(jacobian, probs, root, send_index, count_rows, offset, width):
    count_cols, capacity = send_index.shape
    local_width, all_rows = jacobian.shape
    steps = max(1, min(count_cols, PICK_ROWS // capacity))
    shape = (count_rows, count_cols, capacity, width)
    picks = count_cols * capacity
    return pl.pallas_call(
        functools.partial(pick_kernel, probs.shape[1], offset),
        grid=(count_cols // steps,),
        in_specs=[
            pl.BlockSpec((steps * capacity, 1), lambda t: (t, 0)),
            pl.BlockSpec((all_rows, 1), lambda t: (0, 0)),
            pl.BlockSpec((1, all_rows), lambda t: (0, 0)),
            pl.BlockSpec((local_width, all_rows), lambda t: (0, 0)),
        ],
        out_specs=pl.BlockSpec((count_rows, steps, capacity, width), lambda t: (0, t, 0, 0)),
        out_shape=jax.ShapeDtypeStruct(shape, jnp.bfloat16),
        scratch_shapes=[pltpu.VMEM((3, count_rows, width, width), jnp.bfloat16)],
        cost_estimate=pl.CostEstimate(
            flops=2 * picks * local_width * width * count_rows,
            bytes_accessed=2 * local_width * all_rows + 2 * picks * width * count_rows,
            transcendentals=0,
        ),
        compiler_params=pltpu.CompilerParams(vmem_limit_bytes=VMEM_LIMIT),
    )(send_index.reshape(-1, 1), probs.reshape(all_rows, 1), root.reshape(1, all_rows), jacobian)


def product_kernel(chunks, offset_ref, *refs):
    slabs, tiles, out_ref = refs[:chunks], refs[chunks:-1], refs[-1]
    count = slabs[0].shape[0]
    total = None
    for c, slab in enumerate(slabs):
        for d in range(count):
            part = lax.dot_general(
                slab[d],
                tiles[c * count + d][...],
                (((1,), (1,)), ((), ())),
                preferred_element_type=jnp.float32,
            )
            total = part if total is None else total + part
    rows = offset_ref[0] + lax.broadcasted_iota(jnp.int32, out_ref.shape, 0)
    columns = (
        offset_ref[1]
        + pl.program_id(0) * out_ref.shape[1]
        + lax.broadcasted_iota(jnp.int32, out_ref.shape, 1)
    )
    out_ref[...] = jnp.where(columns <= rows, total, 0.0)


def product(slabs, tiles, offsets, tile_width):
    block = 512
    return pl.pallas_call(
        functools.partial(product_kernel, len(slabs)),
        grid=(tile_width // block,),
        in_specs=[pl.BlockSpec(memory_space=pltpu.SMEM)]
        + [pl.BlockSpec(slab.shape, lambda i: (0, 0, 0)) for slab in slabs]
        + [pl.BlockSpec((block, tile.shape[1]), lambda i: (i, 0)) for tile in tiles],
        out_specs=pl.BlockSpec((SLAB_DEV, block), lambda i: (0, i)),
        out_shape=jax.ShapeDtypeStruct((SLAB_DEV, tile_width), jnp.float32),
        compiler_params=pltpu.CompilerParams(vmem_limit_bytes=VMEM_LIMIT),
    )(offsets, *slabs, *tiles)


def exchange(x, count, d):
    return lax.ppermute(x, "gr", [(i, i ^ d) for i in range(count)])


def gather_pieces(block, count, gate):
    if count != 4:
        return [block] + [exchange(block, count, d) for d in range(1, count)], gate
    half = block.shape[0] // 2
    one, two = exchange(block, 4, 1), exchange(block, 4, 2)
    one, two, gate = lax.optimization_barrier((one, two, gate))
    top, bottom = exchange(one[:half], 4, 2), exchange(two[half:], 4, 1)
    return [block, one, two, jnp.concatenate([top, bottom])], gate


def collect_slab(block, count_rows, count_cols, grid_row, grid_col):
    first = block.shape[0] - SLAB_DEV * count_rows
    last = count_cols - 1

    def rows_of(r):
        return lax.dynamic_slice_in_dim(block, first + r * SLAB_DEV, SLAB_DEV, 0)

    own = rows_of(grid_row)
    parts = [jnp.where(grid_col == last, own, jnp.zeros_like(own))]
    for d in range(1, count_rows):
        pairs = [
            (r * count_cols + last, (r ^ d) * count_cols + last) for r in range(count_rows)
        ]
        parts.append(lax.ppermute(rows_of(grid_row ^ d), ("gr", "gc"), pairs))
    slab = jnp.stack(parts)
    return slab


def local(jacobian, class_scores, source):
    count_rows = lax.axis_size("gr")
    count_cols = lax.axis_size("gc")
    grid_row = lax.axis_index("gr")
    grid_col = lax.axis_index("gc")
    myself = grid_row * count_cols + grid_col
    local_width, all_rows = jacobian.shape
    total_weights = source.shape[0]
    tile_width = total_weights // count_cols
    capacity = 3 * (total_weights // (count_cols * count_cols * count_rows)) // 2
    block_rows = all_rows // count_rows
    widths = [block_rows]
    if block_rows % 384 == 0:
        widths = [2 * block_rows // 3, block_rows // 3]
    slab_total = SLAB_DEV * count_rows
    probs = class_scores / jnp.sum(class_scores, axis=1, keepdims=True)
    root = jnp.sqrt(probs)

    tiles = source.reshape(count_cols, tile_width)
    owned = tiles // local_width == myself
    rank = jnp.where(owned, jnp.cumsum(owned.astype(jnp.int32), axis=1) - 1, -1)
    slots = jnp.arange(capacity, dtype=jnp.int32)
    hit = rank[:, None, :] == slots[None, :, None]
    send_index = jnp.sum(jnp.where(hit, (tiles % local_width + 1)[:, None, :], 0), axis=2) - 1

    tile_source = (
        lax.dynamic_slice_in_dim(source, grid_col * tile_width, tile_width, 0) // local_width
    )
    lane_block = 128
    blocks = tile_source.reshape(-1, lane_block)
    place = jnp.arange(lane_block, dtype=jnp.int32)
    earlier = (blocks[:, :, None] == blocks[:, None, :]) & (place[None, :] < place[:, None])
    within = jnp.sum(earlier.astype(jnp.int32), axis=2)
    owner_ids = jnp.arange(count_rows * count_cols, dtype=jnp.int32)
    belongs = (blocks[:, None, :] == owner_ids[None, :, None]).astype(jnp.int32)
    counts = jnp.sum(belongs, axis=2)
    block_ids = jnp.arange(blocks.shape[0], dtype=jnp.int32)
    before = (block_ids[None, :] < block_ids[:, None]).astype(jnp.int32)
    base = jnp.sum(before[:, :, None] * counts[None, :, :], axis=1)
    arrival = (within + jnp.sum(belongs * base[:, :, None], axis=1)).reshape(-1)
    flat_index = tile_source * capacity + arrival

    slab_list, tile_list = [], []
    offset = 0
    for width in widths:
        part = pick_rows(jacobian, probs, root, send_index, count_rows, offset, width)
        offset += width
        incoming = lax.all_to_all(
            part.reshape(-1, capacity, width), ("gr", "gc"), split_axis=0, concat_axis=0, tiled=True
        )
        block = incoming.reshape(-1, width).at[flat_index].get(mode="promise_in_bounds")
        slab_list.append(collect_slab(block, count_rows, count_cols, grid_row, grid_col))
        if len(slab_list) == len(widths):
            block, slab_list = lax.optimization_barrier((block, slab_list))
            slab_list = lax.psum(slab_list, "gc")
            pieces, slab_list = gather_pieces(block, count_rows, slab_list)
        else:
            pieces, _ = gather_pieces(block, count_rows, [])
        tile_list += pieces
    offsets = jnp.stack(
        [total_weights - slab_total + grid_row * SLAB_DEV, grid_col * tile_width]
    ).astype(jnp.int32)
    return product(slab_list, tile_list, offsets, tile_width)


def solution(mesh):
    in_specs = (P(("gr", "gc"), None), P(), P())
    out_specs = P("gr", "gc")
    return jax.shard_map(local, mesh=mesh, in_specs=in_specs, out_specs=out_specs, check_vma=False)
```

```python
import functools

import jax
import jax.numpy as jnp
from jax import lax
from jax.experimental import pallas as pl
from jax.experimental.pallas import tpu as pltpu
from jax.sharding import PartitionSpec as P

SLAB_DEV = 512
PICK_ROWS = 768
VMEM_LIMIT = 48 * 1024 * 1024


def pick_kernel(classes, offset, index_ref, probs_ref, root_ref, jacobian_ref, out_ref, matrix_ref):
    count_rows, steps, capacity, width = out_ref.shape
    local_width, all_rows = jacobian_ref.shape
    spans = [
        slice(r * (all_rows // count_rows) + offset, r * (all_rows // count_rows) + offset + width)
        for r in range(count_rows)
    ]

    @pl.when(pl.program_id(0) == 0)
    def _():
        down = lax.broadcasted_iota(jnp.int32, (width, width), 0) // classes
        across = lax.broadcasted_iota(jnp.int32, (width, width), 1) // classes
        for r, span in enumerate(spans):
            exact = jnp.where(down == across, probs_ref[span], 0.0)
            for part in range(3):
                piece = exact.astype(jnp.bfloat16)
                matrix_ref[part, r] = piece
                exact = exact - piece.astype(jnp.float32)

    lanes = lax.broadcasted_iota(jnp.int32, (steps * capacity, local_width), 1)
    onehot = jnp.where(lanes == index_ref[...], 1.0, 0.0).astype(jnp.bfloat16)
    for r, span in enumerate(spans):
        values = jnp.dot(onehot, jacobian_ref[:, span], preferred_element_type=jnp.float32)
        short = values.astype(jnp.bfloat16)
        centre = jnp.dot(short, matrix_ref[2, r], preferred_element_type=jnp.float32)
        centre += jnp.dot(short, matrix_ref[1, r], preferred_element_type=jnp.float32)
        centre += jnp.dot(short, matrix_ref[0, r], preferred_element_type=jnp.float32)
        weighted = (root_ref[:, span] * (values - centre)).astype(jnp.bfloat16)
        for t in range(steps):
            out_ref[r, t] = weighted[t * capacity : (t + 1) * capacity]


def pick_rows(jacobian, probs, root, send_index, count_rows, offset, width):
    count_cols, capacity = send_index.shape
    local_width, all_rows = jacobian.shape
    steps = max(1, min(count_cols, PICK_ROWS // capacity))
    shape = (count_rows, count_cols, capacity, width)
    picks = count_cols * capacity
    return pl.pallas_call(
        functools.partial(pick_kernel, probs.shape[1], offset),
        grid=(count_cols // steps,),
        in_specs=[
            pl.BlockSpec((steps * capacity, 1), lambda t: (t, 0)),
            pl.BlockSpec((all_rows, 1), lambda t: (0, 0)),
            pl.BlockSpec((1, all_rows), lambda t: (0, 0)),
            pl.BlockSpec((local_width, all_rows), lambda t: (0, 0)),
        ],
        out_specs=pl.BlockSpec((count_rows, steps, capacity, width), lambda t: (0, t, 0, 0)),
        out_shape=jax.ShapeDtypeStruct(shape, jnp.bfloat16),
        scratch_shapes=[pltpu.VMEM((3, count_rows, width, width), jnp.bfloat16)],
        cost_estimate=pl.CostEstimate(
            flops=2 * picks * local_width * width * count_rows,
            bytes_accessed=2 * local_width * all_rows + 2 * picks * width * count_rows,
            transcendentals=0,
        ),
        compiler_params=pltpu.CompilerParams(vmem_limit_bytes=VMEM_LIMIT),
    )(send_index.reshape(-1, 1), probs.reshape(all_rows, 1), root.reshape(1, all_rows), jacobian)


def product_kernel(chunks, offset_ref, *refs):
    slabs, tiles, out_ref = refs[:chunks], refs[chunks:-1], refs[-1]
    count = slabs[0].shape[0]
    total = None
    for c, slab in enumerate(slabs):
        for d in range(count):
            part = lax.dot_general(
                slab[d],
                tiles[c * count + d][...],
                (((1,), (1,)), ((), ())),
                preferred_element_type=jnp.float32,
            )
            total = part if total is None else total + part
    rows = offset_ref[0] + lax.broadcasted_iota(jnp.int32, out_ref.shape, 0)
    columns = (
        offset_ref[1]
        + pl.program_id(0) * out_ref.shape[1]
        + lax.broadcasted_iota(jnp.int32, out_ref.shape, 1)
    )
    out_ref[...] = jnp.where(columns <= rows, total, 0.0)


def product(slabs, tiles, offsets, tile_width):
    block = 512
    return pl.pallas_call(
        functools.partial(product_kernel, len(slabs)),
        grid=(tile_width // block,),
        in_specs=[pl.BlockSpec(memory_space=pltpu.SMEM)]
        + [pl.BlockSpec(slab.shape, lambda i: (0, 0, 0)) for slab in slabs]
        + [pl.BlockSpec((block, tile.shape[1]), lambda i: (i, 0)) for tile in tiles],
        out_specs=pl.BlockSpec((SLAB_DEV, block), lambda i: (0, i)),
        out_shape=jax.ShapeDtypeStruct((SLAB_DEV, tile_width), jnp.float32),
        compiler_params=pltpu.CompilerParams(vmem_limit_bytes=VMEM_LIMIT),
    )(offsets, *slabs, *tiles)


def exchange(x, count, d):
    return lax.ppermute(x, "gr", [(i, i ^ d) for i in range(count)])


def gather_pieces(block, count, gate):
    if count != 4:
        return [block] + [exchange(block, count, d) for d in range(1, count)], gate
    half = block.shape[0] // 2
    one, two = exchange(block, 4, 1), exchange(block, 4, 2)
    one, two, gate = lax.optimization_barrier((one, two, gate))
    top, bottom = exchange(one[:half], 4, 2), exchange(two[half:], 4, 1)
    return [block, one, two, jnp.concatenate([top, bottom])], gate


def collect_slab(block, count_rows, count_cols, grid_row, grid_col):
    first = block.shape[0] - SLAB_DEV * count_rows
    last = count_cols - 1

    def rows_of(r):
        return lax.dynamic_slice_in_dim(block, first + r * SLAB_DEV, SLAB_DEV, 0)

    own = rows_of(grid_row)
    parts = [jnp.where(grid_col == last, own, jnp.zeros_like(own))]
    for d in range(1, count_rows):
        pairs = [
            (r * count_cols + last, (r ^ d) * count_cols + last) for r in range(count_rows)
        ]
        parts.append(lax.ppermute(rows_of(grid_row ^ d), ("gr", "gc"), pairs))
    slab = jnp.stack(parts)
    return slab


def local(jacobian, class_scores, source):
    count_rows = lax.axis_size("gr")
    count_cols = lax.axis_size("gc")
    grid_row = lax.axis_index("gr")
    grid_col = lax.axis_index("gc")
    myself = grid_row * count_cols + grid_col
    local_width, all_rows = jacobian.shape
    total_weights = source.shape[0]
    tile_width = total_weights // count_cols
    capacity = 3 * (total_weights // (count_cols * count_cols * count_rows)) // 2
    block_rows = all_rows // count_rows
    widths = [block_rows]
    if block_rows % 384 == 0:
        widths = [2 * block_rows // 3, block_rows // 3]
    slab_total = SLAB_DEV * count_rows
    probs = class_scores / jnp.sum(class_scores, axis=1, keepdims=True)
    root = jnp.sqrt(probs)

    tiles = source.reshape(count_cols, tile_width)
    owned = tiles // local_width == myself
    rank = jnp.where(owned, jnp.cumsum(owned.astype(jnp.int32), axis=1) - 1, -1)
    slots = jnp.arange(capacity, dtype=jnp.int32)
    hit = rank[:, None, :] == slots[None, :, None]
    send_index = jnp.sum(jnp.where(hit, (tiles % local_width + 1)[:, None, :], 0), axis=2) - 1

    tile_source = (
        lax.dynamic_slice_in_dim(source, grid_col * tile_width, tile_width, 0) // local_width
    )
    lane_block = 128
    blocks = tile_source.reshape(-1, lane_block)
    place = jnp.arange(lane_block, dtype=jnp.int32)
    earlier = (blocks[:, :, None] == blocks[:, None, :]) & (place[None, :] < place[:, None])
    within = jnp.sum(earlier.astype(jnp.int32), axis=2)
    owner_ids = jnp.arange(count_rows * count_cols, dtype=jnp.int32)
    belongs = (blocks[:, None, :] == owner_ids[None, :, None]).astype(jnp.int32)
    counts = jnp.sum(belongs, axis=2)
    block_ids = jnp.arange(blocks.shape[0], dtype=jnp.int32)
    before = (block_ids[None, :] < block_ids[:, None]).astype(jnp.int32)
    base = jnp.sum(before[:, :, None] * counts[None, :, :], axis=1)
    arrival = (within + jnp.sum(belongs * base[:, :, None], axis=1)).reshape(-1)
    flat_index = tile_source * capacity + arrival

    slab_list, tile_list = [], []
    offset = 0
    for width in widths:
        part = pick_rows(jacobian, probs, root, send_index, count_rows, offset, width)
        offset += width
        incoming = lax.all_to_all(
            part.reshape(-1, capacity, width), ("gr", "gc"), split_axis=0, concat_axis=0, tiled=True
        )
        block = incoming.reshape(-1, width).at[flat_index].get(mode="promise_in_bounds")
        slab = collect_slab(block, count_rows, count_cols, grid_row, grid_col)
        block, slab, slab_list = lax.optimization_barrier((block, slab, slab_list))
        slab_list.append(lax.psum(slab, "gc"))
        if len(slab_list) == len(widths):
            pieces, slab_list = gather_pieces(block, count_rows, slab_list)
        else:
            pieces, _ = gather_pieces(block, count_rows, [])
        tile_list += pieces
    offsets = jnp.stack(
        [total_weights - slab_total + grid_row * SLAB_DEV, grid_col * tile_width]
    ).astype(jnp.int32)
    return product(slab_list, tile_list, offsets, tile_width)


def solution(mesh):
    in_specs = (P(("gr", "gc"), None), P(), P())
    out_specs = P("gr", "gc")
    return jax.shard_map(local, mesh=mesh, in_specs=in_specs, out_specs=out_specs, check_vma=False)
```

```python
import functools

import jax
import jax.numpy as jnp
from jax import lax
from jax.experimental import pallas as pl
from jax.experimental.pallas import tpu as pltpu
from jax.sharding import PartitionSpec as P

SLAB_DEV = 512
PICK_ROWS = 768
VMEM_LIMIT = 48 * 1024 * 1024


def pick_kernel(classes, offset, index_ref, probs_ref, root_ref, jacobian_ref, out_ref, matrix_ref):
    count_rows, steps, capacity, width = out_ref.shape
    local_width, all_rows = jacobian_ref.shape
    spans = [
        slice(r * (all_rows // count_rows) + offset, r * (all_rows // count_rows) + offset + width)
        for r in range(count_rows)
    ]

    @pl.when(pl.program_id(0) == 0)
    def _():
        down = lax.broadcasted_iota(jnp.int32, (width, width), 0) // classes
        across = lax.broadcasted_iota(jnp.int32, (width, width), 1) // classes
        for r, span in enumerate(spans):
            exact = jnp.where(down == across, probs_ref[span], 0.0)
            for part in range(3):
                piece = exact.astype(jnp.bfloat16)
                matrix_ref[part, r] = piece
                exact = exact - piece.astype(jnp.float32)

    lanes = lax.broadcasted_iota(jnp.int32, (steps * capacity, local_width), 1)
    onehot = jnp.where(lanes == index_ref[...], 1.0, 0.0).astype(jnp.bfloat16)
    for r, span in enumerate(spans):
        values = jnp.dot(onehot, jacobian_ref[:, span], preferred_element_type=jnp.float32)
        short = values.astype(jnp.bfloat16)
        centre = jnp.dot(short, matrix_ref[2, r], preferred_element_type=jnp.float32)
        centre += jnp.dot(short, matrix_ref[1, r], preferred_element_type=jnp.float32)
        centre += jnp.dot(short, matrix_ref[0, r], preferred_element_type=jnp.float32)
        weighted = (root_ref[:, span] * (values - centre)).astype(jnp.bfloat16)
        for t in range(steps):
            out_ref[r, t] = weighted[t * capacity : (t + 1) * capacity]


def pick_rows(jacobian, probs, root, send_index, count_rows, offset, width):
    count_cols, capacity = send_index.shape
    local_width, all_rows = jacobian.shape
    steps = max(1, min(count_cols, PICK_ROWS // capacity))
    shape = (count_rows, count_cols, capacity, width)
    picks = count_cols * capacity
    return pl.pallas_call(
        functools.partial(pick_kernel, probs.shape[1], offset),
        grid=(count_cols // steps,),
        in_specs=[
            pl.BlockSpec((steps * capacity, 1), lambda t: (t, 0)),
            pl.BlockSpec((all_rows, 1), lambda t: (0, 0)),
            pl.BlockSpec((1, all_rows), lambda t: (0, 0)),
            pl.BlockSpec((local_width, all_rows), lambda t: (0, 0)),
        ],
        out_specs=pl.BlockSpec((count_rows, steps, capacity, width), lambda t: (0, t, 0, 0)),
        out_shape=jax.ShapeDtypeStruct(shape, jnp.bfloat16),
        scratch_shapes=[pltpu.VMEM((3, count_rows, width, width), jnp.bfloat16)],
        cost_estimate=pl.CostEstimate(
            flops=2 * picks * local_width * width * count_rows,
            bytes_accessed=2 * local_width * all_rows + 2 * picks * width * count_rows,
            transcendentals=0,
        ),
        compiler_params=pltpu.CompilerParams(vmem_limit_bytes=VMEM_LIMIT),
    )(send_index.reshape(-1, 1), probs.reshape(all_rows, 1), root.reshape(1, all_rows), jacobian)


def product_kernel(chunks, offset_ref, *refs):
    slabs, tiles, out_ref = refs[:chunks], refs[chunks:-1], refs[-1]
    count = slabs[0].shape[0]
    total = None
    for c, slab in enumerate(slabs):
        for d in range(count):
            part = lax.dot_general(
                slab[d],
                tiles[c * count + d][...],
                (((1,), (1,)), ((), ())),
                preferred_element_type=jnp.float32,
            )
            total = part if total is None else total + part
    rows = offset_ref[0] + lax.broadcasted_iota(jnp.int32, out_ref.shape, 0)
    columns = (
        offset_ref[1]
        + pl.program_id(0) * out_ref.shape[1]
        + lax.broadcasted_iota(jnp.int32, out_ref.shape, 1)
    )
    out_ref[...] = jnp.where(columns <= rows, total, 0.0)


def product(slabs, tiles, offsets, tile_width):
    block = 512
    return pl.pallas_call(
        functools.partial(product_kernel, len(slabs)),
        grid=(tile_width // block,),
        in_specs=[pl.BlockSpec(memory_space=pltpu.SMEM)]
        + [pl.BlockSpec(slab.shape, lambda i: (0, 0, 0)) for slab in slabs]
        + [pl.BlockSpec((block, tile.shape[1]), lambda i: (i, 0)) for tile in tiles],
        out_specs=pl.BlockSpec((SLAB_DEV, block), lambda i: (0, i)),
        out_shape=jax.ShapeDtypeStruct((SLAB_DEV, tile_width), jnp.float32),
        compiler_params=pltpu.CompilerParams(vmem_limit_bytes=VMEM_LIMIT),
    )(offsets, *slabs, *tiles)


def exchange(x, count, d):
    return lax.ppermute(x, "gr", [(i, i ^ d) for i in range(count)])


def gather_pieces(block, count, gate):
    if count != 4:
        return [block] + [exchange(block, count, d) for d in range(1, count)], gate
    half = block.shape[0] // 2
    one, two = exchange(block, 4, 1), exchange(block, 4, 2)
    one, two, gate = lax.optimization_barrier((one, two, gate))
    top, bottom = exchange(one[:half], 4, 2), exchange(two[half:], 4, 1)
    return [block, one, two, jnp.concatenate([top, bottom])], gate


def collect_slab(block, count_rows, count_cols, grid_row, grid_col):
    first = block.shape[0] - SLAB_DEV * count_rows
    last = count_cols - 1

    def rows_of(r):
        return lax.dynamic_slice_in_dim(block, first + r * SLAB_DEV, SLAB_DEV, 0)

    own = rows_of(grid_row)
    parts = [jnp.where(grid_col == last, own, jnp.zeros_like(own))]
    for d in range(1, count_rows):
        pairs = [
            (r * count_cols + last, (r ^ d) * count_cols + last) for r in range(count_rows)
        ]
        parts.append(lax.ppermute(rows_of(grid_row ^ d), ("gr", "gc"), pairs))
    slab = jnp.stack(parts)
    return slab


def double_slab(slab, count_cols):
    stride = count_cols // 2
    while stride:
        pairs = [(c, c - stride) for c in range(count_cols - 1, 0, -2 * stride)]
        slab = slab + lax.ppermute(slab, "gc", pairs)
        stride //= 2
    return slab


def local(jacobian, class_scores, source):
    count_rows = lax.axis_size("gr")
    count_cols = lax.axis_size("gc")
    grid_row = lax.axis_index("gr")
    grid_col = lax.axis_index("gc")
    myself = grid_row * count_cols + grid_col
    local_width, all_rows = jacobian.shape
    total_weights = source.shape[0]
    tile_width = total_weights // count_cols
    capacity = 3 * (total_weights // (count_cols * count_cols * count_rows)) // 2
    block_rows = all_rows // count_rows
    widths = [block_rows]
    if block_rows % 384 == 0:
        widths = [2 * block_rows // 3, block_rows // 3]
    slab_total = SLAB_DEV * count_rows
    probs = class_scores / jnp.sum(class_scores, axis=1, keepdims=True)
    root = jnp.sqrt(probs)

    tiles = source.reshape(count_cols, tile_width)
    owned = tiles // local_width == myself
    rank = jnp.where(owned, jnp.cumsum(owned.astype(jnp.int32), axis=1) - 1, -1)
    slots = jnp.arange(capacity, dtype=jnp.int32)
    hit = rank[:, None, :] == slots[None, :, None]
    send_index = jnp.sum(jnp.where(hit, (tiles % local_width + 1)[:, None, :], 0), axis=2) - 1

    tile_source = (
        lax.dynamic_slice_in_dim(source, grid_col * tile_width, tile_width, 0) // local_width
    )
    lane_block = 128
    blocks = tile_source.reshape(-1, lane_block)
    place = jnp.arange(lane_block, dtype=jnp.int32)
    earlier = (blocks[:, :, None] == blocks[:, None, :]) & (place[None, :] < place[:, None])
    within = jnp.sum(earlier.astype(jnp.int32), axis=2)
    owner_ids = jnp.arange(count_rows * count_cols, dtype=jnp.int32)
    belongs = (blocks[:, None, :] == owner_ids[None, :, None]).astype(jnp.int32)
    counts = jnp.sum(belongs, axis=2)
    block_ids = jnp.arange(blocks.shape[0], dtype=jnp.int32)
    before = (block_ids[None, :] < block_ids[:, None]).astype(jnp.int32)
    base = jnp.sum(before[:, :, None] * counts[None, :, :], axis=1)
    arrival = (within + jnp.sum(belongs * base[:, :, None], axis=1)).reshape(-1)
    flat_index = tile_source * capacity + arrival

    slab_list, tile_list = [], []
    offset = 0
    for width in widths:
        part = pick_rows(jacobian, probs, root, send_index, count_rows, offset, width)
        offset += width
        incoming = lax.all_to_all(
            part.reshape(-1, capacity, width), ("gr", "gc"), split_axis=0, concat_axis=0, tiled=True
        )
        block = incoming.reshape(-1, width).at[flat_index].get(mode="promise_in_bounds")
        slab_list.append(collect_slab(block, count_rows, count_cols, grid_row, grid_col))
        if len(slab_list) == len(widths):
            block, slab_list = lax.optimization_barrier((block, slab_list))
            slab_list = [double_slab(slab, count_cols) for slab in slab_list]
            pieces, _ = gather_pieces(block, count_rows, [])
        else:
            pieces, _ = gather_pieces(block, count_rows, [])
        tile_list += pieces
    offsets = jnp.stack(
        [total_weights - slab_total + grid_row * SLAB_DEV, grid_col * tile_width]
    ).astype(jnp.int32)
    return product(slab_list, tile_list, offsets, tile_width)


def solution(mesh):
    in_specs = (P(("gr", "gc"), None), P(), P())
    out_specs = P("gr", "gc")
    return jax.shard_map(local, mesh=mesh, in_specs=in_specs, out_specs=out_specs, check_vma=False)
```
